32 devices in a mesh: blk: 32 (over z, y, x, core).
Axes of the slice: x: 2, y: 2, z: 4, core: 2. Of those that a mesh axis runs over, the one named last changes fastest.
Arguments:
- f_coarse: float32 [64, 27, 512], P('blk'), as said below
- f_mid: float32 [128, 27, 512], P('blk'), as said below
- f_fine: float32 [256, 27, 512], P('blk'), as said below
- solid_coarse: float32 [64, 512], P('blk'), may hold values from 0 to 0.7
- solid_mid: float32 [128, 512], P('blk'), may hold values from 0 to 0.7
- solid_fine: float32 [256, 512], P('blk'), may hold values from 0 to 0.7
- rates: float32 [3, 27], replicated, may hold values from 0.6 to 1.8
- faces_coarse: int32 [64, 6], P('blk'), may hold values from -1 to 63, as said below
- faces_mid: int32 [128, 6], P('blk'), may hold values from -1 to 127, as said below
- faces_fine: int32 [256, 6], P('blk'), may hold values from -1 to 255, as said below
- explode_mid: int32 [128, 2], P('blk'), may hold values from -1 to 63, as said below
- explode_fine: int32 [256, 2], P('blk'), may hold values from -1 to 127, as said below
- coalesce_coarse: int32 [64, 8], P('blk'), may hold values from -1 to 127, as said below
- coalesce_mid: int32 [128, 8], P('blk'), may hold values from -1 to 255, as said below
Outputs:
- coarse_out: float32 [64, 27, 512], P('blk')
- mid_out: float32 [128, 27, 512], P('blk')
- fine_out: float32 [256, 27, 512], P('blk')
The draws below stay inside these ranges and needn't reach their ends.
Inputs may be any that keep to these rules, and one draw needn't show every extreme that they name: `faces_coarse`: block g of a level with 2 blocks a group lies in group g // 2; every named block lies in the same group as g or in one of the two beside it, and some block names the group below and some the group above. `faces_mid`: likewise with 4 blocks a group. `faces_fine`: likewise with 8 blocks a group. `explode_mid`: column 0 is a coarse block or -1, lying in group q // 4 of its own level counted in groups of 2 blocks, or one beside it; column 1 is an octant 0 to 7. `explode_fine`: column 0 is a middle-level block or -1, in the group q // 8 counted in groups of 4 blocks, or one beside it; column 1 is an octant 0 to 7. `coalesce_coarse`: each entry is a middle-level block or -1, in group p // 2 counted in groups of 4 blocks, or one beside it. `coalesce_mid`: each entry is a fine block or -1, in group p // 4 counted in groups of 8 blocks, or one beside it. `f_coarse`: positive in every entry. `f_mid`: positive in every entry. `f_fine`: positive in every entry.
All inputs are finite; a program needn't handle non-finite values.
Results may differ from the reference program's by a relative error of at most 0.0001.
Values sent between devices are 32-bit elements; how exact they have to be, the bound alone decides.
A program may use at most 512 MiB of HBM per device.

```python
import jax
import jax.numpy as jnp
from jax import lax

C = 8
S = 512
B0 = 2
B1 = 4
B2 = 8
NB0 = 64
NB1 = 128
NB2 = 256
N_BLK = 32


def populations(key, count, rho_lo, rho_hi, speed, rough):
    cells = C ** 3
    k_rho, k_vel, k_noise = jax.random.split(key, 3)
    density = jax.random.uniform(k_rho, (count, 1, cells), jnp.float32, rho_lo, rho_hi)
    velocity = jax.random.uniform(k_vel, (count, 3, cells), jnp.float32, -speed, speed)
    square = velocity * velocity
    weights = jnp.stack([(1.0 / 3.0 + square - velocity) * 0.5, 2.0 / 3.0 - square, (1.0 / 3.0 + square + velocity) * 0.5], axis=2)
    base = weights[:, 0][:, :, None, None, :] * weights[:, 1][:, None, :, None, :] * weights[:, 2][:, None, None, :, :]
    base = base.reshape(count, 27, cells)
    noise = jax.random.uniform(k_noise, (count, 27, cells), jnp.float32, -rough, rough)
    return density * base * (1.0 + noise)


def nearby(key, rows, own, cols, other):
    k_step, k_slot, k_gap = jax.random.split(key, 3)
    index = jnp.arange(rows, dtype=jnp.int32)
    device = (index // own)[:, None]
    slot = (index % own)[:, None]
    column = jnp.arange(cols, dtype=jnp.int32)[None, :]
    pick = jax.random.randint(k_step, (rows, cols), 0, 5)
    step = jnp.where(pick == 3, -1, jnp.where(pick == 4, 1, 0))
    lower = (slot == 0) & (column == 0) & (device > 0)
    upper = (slot == own - 1) & (column == cols - 1) & (device < N_BLK - 1)
    step = jnp.where(lower, -1, jnp.where(upper, 1, step))
    target = jnp.clip(device + step, 0, N_BLK - 1)
    ident = target * other + jax.random.randint(k_slot, (rows, cols), 0, other)
    empty = (jax.random.randint(k_gap, (rows, cols), 0, 10) < 3) & ~lower & ~upper
    return jnp.where(empty, -1, ident).astype(jnp.int32)


def with_octant(key, rows, own, other):
    k_ids, k_oct = jax.random.split(key)
    ident = nearby(k_ids, rows, own, 1, other)
    octant = jax.random.randint(k_oct, (rows, 1), 0, 8).astype(jnp.int32)
    return jnp.concatenate([ident, octant], axis=1)


def draw_f_coarse(key, part):
    key = jax.random.fold_in(key, 1)
    return populations(key, NB0, 0.85, 1.2, 0.12, 0.2)


def draw_f_mid(key, part):
    key = jax.random.fold_in(key, 2)
    return populations(key, NB1, 0.85, 1.2, 0.12, 0.2)


def draw_f_fine(key, part):
    key = jax.random.fold_in(key, 3)
    return populations(key, NB2, 0.85, 1.2, 0.12, 0.2)


def draw_faces_coarse(key, part):
    key = jax.random.fold_in(key, 4)
    return nearby(key, NB0, B0, 6, B0)


def draw_faces_mid(key, part):
    key = jax.random.fold_in(key, 5)
    return nearby(key, NB1, B1, 6, B1)


def draw_faces_fine(key, part):
    key = jax.random.fold_in(key, 6)
    return nearby(key, NB2, B2, 6, B2)


def draw_explode_mid(key, part):
    key = jax.random.fold_in(key, 7)
    return with_octant(key, NB1, B1, B0)


def draw_explode_fine(key, part):
    key = jax.random.fold_in(key, 8)
    return with_octant(key, NB2, B2, B1)


def draw_coalesce_coarse(key, part):
    key = jax.random.fold_in(key, 9)
    return nearby(key, NB0, B0, 8, B1)


def draw_coalesce_mid(key, part):
    key = jax.random.fold_in(key, 10)
    return nearby(key, NB1, B1, 8, B2)


def levels(stream_key, extent, shards, low, largest):
    gain = 1.0
    for axis_at, shards_of in shards:
        draws = jax.random.uniform(jax.random.fold_in(jax.random.fold_in(stream_key, 6), axis_at), (shards_of,), jnp.float32, low / len(shards), largest / len(shards))
        gain = gain * jnp.repeat(jnp.exp(draws), extent[axis_at] // shards_of).reshape((-1,) + (1,) * (len(extent) - 1 - axis_at))
    return gain


def setup_inputs(seed: int = 0) -> dict:
    key_of = jax.random.split(jax.random.key(seed), 15)
    return {
        "f_coarse": draw_f_coarse(jax.random.fold_in(key_of[14], 71), 0),
        "f_mid": draw_f_mid(jax.random.fold_in(key_of[14], 71), 0),
        "f_fine": draw_f_fine(jax.random.fold_in(key_of[14], 71), 0),
        "solid_coarse": jnp.clip(0.7 * jax.random.uniform(key_of[3], (NB0, S), jnp.float32) ** levels(key_of[3], (NB0, S), ((0, 32),), -0.2, 0.2), 0.0, 0.7),
        "solid_mid": jnp.clip(0.7 * jax.random.uniform(key_of[4], (NB1, S), jnp.float32) ** levels(key_of[4], (NB1, S), ((0, 32),), -0.2, 0.2), 0.0, 0.7),
        "solid_fine": jnp.clip(0.7 * jax.random.uniform(key_of[5], (NB2, S), jnp.float32) ** levels(key_of[5], (NB2, S), ((0, 32),), -0.2, 0.2), 0.0, 0.7),
        "rates": jnp.clip(jax.random.uniform(key_of[6], (3, 27), jnp.float32, 0.6, 1.8), 0.6, 1.8),
        "faces_coarse": draw_faces_coarse(jax.random.fold_in(key_of[14], 71), 0),
        "faces_mid": draw_faces_mid(jax.random.fold_in(key_of[14], 71), 0),
        "faces_fine": draw_faces_fine(jax.random.fold_in(key_of[14], 71), 0),
        "explode_mid": draw_explode_mid(jax.random.fold_in(key_of[14], 71), 0),
        "explode_fine": draw_explode_fine(jax.random.fold_in(key_of[14], 71), 0),
        "coalesce_coarse": draw_coalesce_coarse(jax.random.fold_in(key_of[14], 71), 0),
        "coalesce_mid": draw_coalesce_mid(jax.random.fold_in(key_of[14], 71), 0),
    }


HIGH = lax.Precision.HIGHEST
V_ROWS = ((1.0, 1.0, 1.0), (-1.0, 0.0, 1.0), (1.0, 0.0, 1.0))
V_BACK = ((0.0, -0.5, 0.5), (1.0, 0.0, -1.0), (0.0, 0.5, 0.5))


def separable(field, table):
    matrix = jnp.asarray(table, jnp.float32)
    count = field.shape[0]
    cells = field.shape[-1]
    grid = field.reshape(count, 3, 3, 3, cells)
    grid = jnp.einsum('ai,nijks->najks', matrix, grid, precision=HIGH)
    grid = jnp.einsum('bj,najks->nabks', matrix, grid, precision=HIGH)
    grid = jnp.einsum('ck,nabks->nabcs', matrix, grid, precision=HIGH)
    return grid.reshape(count, 27, cells)


def moment_terms(speed):
    return jnp.stack([jnp.ones_like(speed), speed, 1.0 / 3.0 + speed * speed], axis=1)


def relax(moments, solid, rate):
    density = moments[:, 0]
    keep = (1.0 - solid) / density
    along_x = moment_terms(moments[:, 9] * keep)
    along_y = moment_terms(moments[:, 3] * keep)
    along_z = moment_terms(moments[:, 1] * keep)
    target = density[:, None, None, None, :] * along_x[:, :, None, None, :] * along_y[:, None, :, None, :] * along_z[:, None, None, :, :]
    target = target.reshape(moments.shape)
    return moments - rate[None, :, None] * (moments - target)


def collide(field, solid, rate):
    return separable(relax(separable(field, V_ROWS), solid, rate), V_BACK)


def split_velocity(field, axis, edge):
    grid = field.reshape((field.shape[0], 3, 3, 3, edge, edge, edge))
    return [lax.index_in_dim(grid, k, 1 + axis, keepdims=False) for k in range(3)]


def layer(part, index, axis):
    face = lax.index_in_dim(part, index, 3 + axis, keepdims=False)
    return face.reshape(face.shape[0], 9, -1)


def edges(field, axis, edge):
    minus, rest, plus = split_velocity(field, axis, edge)
    return layer(plus, edge - 1, axis), layer(minus, 0, axis), layer(plus, 0, axis), layer(minus, edge - 1, axis)


def stream(field, axis, edge, into_low, into_high):
    minus, rest, plus = split_velocity(field, axis, edge)
    spot = 3 + axis
    count = field.shape[0]
    low = jnp.expand_dims(into_low.reshape(count, 3, 3, edge, edge), spot)
    high = jnp.expand_dims(into_high.reshape(count, 3, 3, edge, edge), spot)
    plus = jnp.concatenate([low, lax.slice_in_dim(plus, 0, edge - 1, axis=spot)], axis=spot)
    minus = jnp.concatenate([lax.slice_in_dim(minus, 1, edge, axis=spot), high], axis=spot)
    grid = jnp.stack([minus, rest, plus], axis=1 + axis)
    return grid.reshape(count, 27, edge ** 3)


def stream_level(field, table, edge):
    for axis in range(3):
        sent_high, sent_low, own_low, own_high = edges(field, axis, edge)
        low_id = table[:, 2 * axis]
        high_id = table[:, 2 * axis + 1]
        into_low = jnp.where((low_id >= 0)[:, None, None], sent_high[jnp.maximum(low_id, 0)], own_low)
        into_high = jnp.where((high_id >= 0)[:, None, None], sent_low[jnp.maximum(high_id, 0)], own_high)
        field = stream(field, axis, edge, into_low, into_high)
    return field


def advance(field, solid, rate, table, count, edge):
    for step in range(count):
        field = collide(field, solid, rate)
        field = stream_level(field, table, edge)
    return field


def octant_table(blocks, edge):
    half = edge // 2
    count = blocks.shape[0]
    grid = blocks.reshape(count, 27, 2, half, 2, half, 2, half).transpose(0, 2, 4, 6, 1, 3, 5, 7)
    return grid.reshape(count * 8, 27, half ** 3)


def rim_mask(edge):
    line = jnp.arange(edge)
    side = (line == 0) | (line == edge - 1)
    return (side[:, None, None] | side[None, :, None] | side[None, None, :]).reshape(edge ** 3)


def explode(child, pieces, parent_id, edge):
    half = edge // 2
    count = child.shape[0]
    grid = pieces.reshape(count, 27, half, 1, half, 1, half, 1)
    grid = jnp.broadcast_to(grid, (count, 27, half, 2, half, 2, half, 2)).reshape(count, 27, edge ** 3)
    keep = (parent_id >= 0)[:, None, None] & rim_mask(edge)[None, None, :]
    return jnp.where(keep, grid, child)


def restrict(blocks, edge):
    half = edge // 2
    count = blocks.shape[0]
    grid = blocks.reshape(count, 27, half, 2, half, 2, half, 2)
    return (jnp.sum(grid, axis=(3, 5, 7)) * 0.125).reshape(count, 27, half ** 3)


def assemble(parent, means, child_id, edge):
    half = edge // 2
    count = parent.shape[0]
    grid = parent.reshape(count, 27, 2, half, 2, half, 2, half)
    parts = []
    for octant in range(8):
        old = grid[:, :, octant // 4, :, (octant // 2) % 2, :, octant % 2, :]
        fresh = means[:, octant].reshape(count, 27, half, half, half)
        parts.append(jnp.where((child_id[:, octant] >= 0)[:, None, None, None, None], fresh, old))
    inner = [[jnp.stack([parts[ox * 4 + oy * 2], parts[ox * 4 + oy * 2 + 1]], axis=4) for oy in range(2)] for ox in range(2)]
    middle = [jnp.stack(inner[ox], axis=3) for ox in range(2)]
    return jnp.stack(middle, axis=2).reshape(count, 27, edge ** 3)


def reference(f_coarse, f_mid, f_fine, solid_coarse, solid_mid, solid_fine, rates, faces_coarse, faces_mid, faces_fine, explode_mid, explode_fine, coalesce_coarse, coalesce_mid):
    edge = C

    def pieces_for(parent, table):
        slots = jnp.maximum(table[:, 0], 0) * 8 + table[:, 1]
        return octant_table(parent, edge)[slots]

    mid_start = explode(f_mid, pieces_for(f_coarse, explode_mid), explode_mid[:, 0], edge)
    fine_start = explode(f_fine, pieces_for(f_mid, explode_fine), explode_fine[:, 0], edge)
    coarse = advance(f_coarse, solid_coarse, rates[0], faces_coarse, 1, edge)
    middle = advance(mid_start, solid_mid, rates[1], faces_mid, 2, edge)
    fine_out = advance(fine_start, solid_fine, rates[2], faces_fine, 4, edge)
    coarse_out = assemble(coarse, restrict(middle, edge)[jnp.maximum(coalesce_coarse, 0)], coalesce_coarse, edge)
    mid_out = assemble(middle, restrict(fine_out, edge)[jnp.maximum(coalesce_mid, 0)], coalesce_mid, edge)
    return coarse_out, mid_out, fine_out
```

```python
import functools

import jax
import jax.numpy as jnp
from jax import lax
from jax.experimental import pallas as pl
from jax.experimental.pallas import tpu as pltpu
from jax.sharding import PartitionSpec as P

C = 8


HIGH = lax.Precision.HIGHEST
V_ROWS = ((1.0, 1.0, 1.0), (-1.0, 0.0, 1.0), (1.0, 0.0, 1.0))
V_BACK = ((0.0, -0.5, 0.5), (1.0, 0.0, -1.0), (0.0, 0.5, 0.5))


def padded(array, sides, width):
    for axis, dim in sides:
        peers, length = (lax.axis_size(axis), array.shape[dim])
        up = [(i, (i + 1) % peers) for i in range(peers - 1)]
        down = [(j, i) for i, j in up]
        last = lax.slice_in_dim(array, length - width, length, axis=dim)
        first = lax.slice_in_dim(array, 0, width, axis=dim)
        before = lax.ppermute(last, axis, up)
        after = lax.ppermute(first, axis, down)
        array = jnp.concatenate([before, array, after], axis=dim)
    return array


def separable(field, table):
    matrix = jnp.asarray(table, jnp.float32)
    count = field.shape[0]
    cells = field.shape[-1]
    grid = field.reshape(count, 3, 3, 3, cells)
    grid = jnp.einsum("ai,nijks->najks", matrix, grid, precision=HIGH)
    grid = jnp.einsum("bj,najks->nabks", matrix, grid, precision=HIGH)
    grid = jnp.einsum("ck,nabks->nabcs", matrix, grid, precision=HIGH)
    return grid.reshape(count, 27, cells)


def moment_terms(speed):
    return jnp.stack([jnp.ones_like(speed), speed, 1.0 / 3.0 + speed * speed], axis=1)


def relax(moments, solid, rate):
    density = moments[:, 0]
    keep = (1.0 - solid) / density
    along_x = moment_terms(moments[:, 9] * keep)
    along_y = moment_terms(moments[:, 3] * keep)
    along_z = moment_terms(moments[:, 1] * keep)
    target = (
        density[:, None, None, None, :]
        * along_x[:, :, None, None, :]
        * along_y[:, None, :, None, :]
        * along_z[:, None, None, :, :]
    )
    target = target.reshape(moments.shape)
    return moments - rate[None, :, None] * (moments - target)


def collide(field, solid, rate):
    return separable(relax(separable(field, V_ROWS), solid, rate), V_BACK)


def split_velocity(field, axis, edge):
    grid = field.reshape((field.shape[0], 3, 3, 3, edge, edge, edge))
    return [lax.index_in_dim(grid, k, 1 + axis, keepdims=False) for k in range(3)]


def layer(part, index, axis):
    face = lax.index_in_dim(part, index, 3 + axis, keepdims=False)
    return face.reshape(face.shape[0], 9, -1)


def edges(field, axis, edge):
    minus, rest, plus = split_velocity(field, axis, edge)
    return (
        layer(plus, edge - 1, axis),
        layer(minus, 0, axis),
        layer(plus, 0, axis),
        layer(minus, edge - 1, axis),
    )


def stream(field, axis, edge, into_low, into_high):
    minus, rest, plus = split_velocity(field, axis, edge)
    spot = 3 + axis
    count = field.shape[0]
    low = jnp.expand_dims(into_low.reshape(count, 3, 3, edge, edge), spot)
    high = jnp.expand_dims(into_high.reshape(count, 3, 3, edge, edge), spot)
    plus = jnp.concatenate([low, lax.slice_in_dim(plus, 0, edge - 1, axis=spot)], axis=spot)
    minus = jnp.concatenate([lax.slice_in_dim(minus, 1, edge, axis=spot), high], axis=spot)
    grid = jnp.stack([minus, rest, plus], axis=1 + axis)
    return grid.reshape(count, 27, edge**3)


def settle(field, axis, edge, near, table, lowest, own_low, own_high):
    rows = near.shape[0]
    low_id = table[:, 2 * axis]
    high_id = table[:, 2 * axis + 1]
    low_at = jnp.clip(low_id - lowest, 0, rows - 1)
    high_at = jnp.clip(high_id - lowest, 0, rows - 1)
    into_low = jnp.where((low_id >= 0)[:, None, None], near[low_at, 0], own_low)
    into_high = jnp.where((high_id >= 0)[:, None, None], near[high_at, 1], own_high)
    return stream(field, axis, edge, into_low, into_high)


def octant_table(blocks, edge):
    half = edge // 2
    count = blocks.shape[0]
    grid = blocks.reshape(count, 27, 2, half, 2, half, 2, half).transpose(0, 2, 4, 6, 1, 3, 5, 7)
    return grid.reshape(count * 8, 27, half**3)


def lookup(table, wanted, lowest):
    blocks = table.shape[0] // 8
    slots = jnp.clip(jnp.maximum(wanted[:, 0], 0) - lowest, 0, blocks - 1) * 8 + wanted[:, 1]
    return table[slots]


def rim_mask(edge):
    line = jnp.arange(edge)
    side = (line == 0) | (line == edge - 1)
    return (side[:, None, None] | side[None, :, None] | side[None, None, :]).reshape(edge**3)


def explode(child, pieces, parent_id, edge):
    half = edge // 2
    count = child.shape[0]
    grid = pieces.reshape(count, 27, half, 1, half, 1, half, 1)
    grid = jnp.broadcast_to(grid, (count, 27, half, 2, half, 2, half, 2)).reshape(
        count, 27, edge**3
    )
    keep = (parent_id >= 0)[:, None, None] & rim_mask(edge)[None, None, :]
    return jnp.where(keep, grid, child)


def restrict(blocks, edge):
    half = edge // 2
    count = blocks.shape[0]
    grid = blocks.reshape(count, 27, half, 2, half, 2, half, 2)
    return (jnp.sum(grid, axis=(3, 5, 7)) * 0.125).reshape(count, 27, half**3)


def assemble(parent, means, child_id, edge):
    half = edge // 2
    count = parent.shape[0]
    grid = parent.reshape(count, 27, 2, half, 2, half, 2, half)
    parts = []
    for octant in range(8):
        old = grid[:, :, octant // 4, :, octant // 2 % 2, :, octant % 2, :]
        fresh = means[:, octant].reshape(count, 27, half, half, half)
        parts.append(jnp.where((child_id[:, octant] >= 0)[:, None, None, None, None], fresh, old))
    inner = [
        [jnp.stack([parts[ox * 4 + oy * 2], parts[ox * 4 + oy * 2 + 1]], axis=4) for oy in range(2)]
        for ox in range(2)
    ]
    middle = [jnp.stack(inner[ox], axis=3) for ox in range(2)]
    return jnp.stack(middle, axis=2).reshape(count, 27, edge**3)


def face_block(field, axis, edge):
    sent_high, sent_low, own_low, own_high = edges(field, axis, edge)
    count = field.shape[0]
    sent = jnp.stack([sent_high, sent_low], axis=1).reshape(1, count * 18, -1)
    return (sent, own_low, own_high)


SLOTS = 16
LANES = 128
MESH = pl.DeviceIdType.MESH


def forward(f, stride):
    out = list(f)
    for i in range(27):
        if i // stride % 3 == 0:
            lo, mid, hi = f[i], f[i + stride], f[i + 2 * stride]
            both = lo + hi
            out[i] = both + mid
            out[i + stride] = hi - lo
            out[i + 2 * stride] = both
    return out


def backward(m, stride):
    out = list(m)
    for i in range(27):
        if i // stride % 3 == 0:
            m0, m1, m2 = m[i], m[i + stride], m[i + 2 * stride]
            out[i] = 0.5 * (m2 - m1)
            out[i + stride] = m0 - m2
            out[i + 2 * stride] = 0.5 * (m1 + m2)
    return out


def collide_row(f, keep, rate_ref):
    for stride in (9, 3, 1):
        f = forward(f, stride)
    rho = f[0]
    scale = keep / rho
    mu = []
    for k in (9, 3, 1):
        v = f[k] * scale
        mu.append((None, v, 1.0 / 3.0 + v * v))
    for a in range(3):
        ta = rho if a == 0 else rho * mu[0][a]
        for b in range(3):
            tb = ta if b == 0 else ta * mu[1][b]
            for c in range(3):
                t = tb if c == 0 else tb * mu[2][c]
                i = 9 * a + 3 * b + c
                f[i] = f[i] - rate_ref[i : i + 1, :] * (f[i] - t)
    for stride in (9, 3, 1):
        f = backward(f, stride)
    return f


def pick(v, idx):
    return jnp.take_along_axis(v, idx, axis=1, mode="promise_in_bounds")


def lbm_kernel(
    n, n_fine, n_mid, f_ref, keep_ref, rate_ref, tab_ref, out_ref, P, Q, R, G, snap, S, RV, send_sem, recv_sem
):
    me = lax.axis_index("blk")
    right, left = lax.rem(me + 1, n), lax.rem(me + n - 1, n)
    barrier = pltpu.get_barrier_semaphore()

    @pl.when(me > 0)
    def _():
        pl.semaphore_signal(barrier, inc=1, device_id=(left,), device_id_type=MESH)

    @pl.when(me < n - 1)
    def _():
        pl.semaphore_signal(barrier, inc=1, device_id=(right,), device_id_type=MESH)

    lane = lax.broadcasted_iota(jnp.int32, (8, LANES), 1)
    lane64 = lax.broadcasted_iota(jnp.int32, (64, LANES), 1)
    row64 = lax.broadcasted_iota(jnp.int32, (64, LANES), 0) % 8

    def copies(slot):
        out = []
        for side, target in ((0, right), (1, left)):
            out.append(
                pltpu.make_async_remote_copy(
                    src_ref=S.at[slot],
                    dst_ref=RV.at[slot, side],
                    send_sem=send_sem.at[slot, side],
                    recv_sem=recv_sem.at[slot, side],
                    device_id=(target,),
                    device_id_type=MESH,
                )
            )
        return out

    def send(slot):
        up, down = copies(slot)

        @pl.when(me < n - 1)
        def _():
            up.start()

        @pl.when(me > 0)
        def _():
            down.start()

    def receive(slot):
        up, down = copies(slot)

        @pl.when(me < n - 1)
        def _():
            up.wait_send()
            down.wait_recv()

        @pl.when(me > 0)
        def _():
            down.wait_send()
            up.wait_recv()

    def own(slot, axis):
        for d in range(2):
            idx, dev = tab_ref[4 * axis + 2 * d], tab_ref[4 * axis + 2 * d + 1]
            for j in range(9):
                G[d, j] = jnp.where(dev == 0, pick(S[slot, d, j], idx), G[d, j])

    def merge(slot, axis, d, j):
        idx, dev = tab_ref[4 * axis + 2 * d], tab_ref[4 * axis + 2 * d + 1]
        g = jnp.where(dev == -1, pick(RV[slot, 0, d, j], idx), G[d, j])
        return jnp.where(dev == 1, pick(RV[slot, 1, d, j], idx), g)

    def collide_at(x):
        at = pl.ds(pl.multiple_of(8 * x, 8), 8)
        f = collide_row([R[i, at, :] for i in range(27)], keep_ref[at, :], rate_ref)
        to = pl.ds(pl.multiple_of(8 * x + 8, 8), 8)
        for i in range(27):
            P[i, to, :] = f[i]

    def step_body(step, carry):
        @pl.loop(0, 2)
        def _(k):
            collide_at(7 * k)

        slot = 3 * step
        for j in range(9):
            S[slot, 0, j] = P[18 + j, 64:72, :]
            S[slot, 1, j] = P[j, 8:16, :]

        @pl.when(step == 0)
        def _():
            @pl.when((me == 0) | (me == n - 1))
            def _():
                pl.semaphore_wait(barrier, 1)

            @pl.when((me > 0) & (me < n - 1))
            def _():
                pl.semaphore_wait(barrier, 2)

        send(slot)

        @pl.loop(1, 7)
        def _(x):
            collide_at(x)

        for j in range(9):
            G[0, j] = P[18 + j, 8:16, :]
            G[1, j] = P[j, 64:72, :]
        own(slot, 0)
        receive(slot)
        for j in range(9):
            P[18 + j, 0:8, :] = merge(slot, 0, 0, j)
            P[j, 72:80, :] = merge(slot, 0, 1, j)

        slot = 3 * step + 1
        for j in range(9):
            a, c = j // 3, j % 3
            plus, minus, base = 9 * a + 6 + c, 9 * a + c, 8 * (2 - a)
            S[slot, 0, j] = P[plus, pl.ds(base + 7, 8, stride=8), :]
            S[slot, 1, j] = P[minus, pl.ds(base, 8, stride=8), :]
        send(slot)
        for j in range(9):
            a, c = j // 3, j % 3
            plus, rest, minus, base = 9 * a + 6 + c, 9 * a + 3 + c, 9 * a + c, 8 * (2 - a)
            G[0, j] = P[plus, pl.ds(base, 8, stride=8), :]
            G[1, j] = P[minus, pl.ds(base + 7, 8, stride=8), :]
            Q[rest] = P[rest, base : base + 64, :]
            Q[plus] = pltpu.roll(P[plus, base : base + 64, :], 1, 0)
            Q[minus] = pltpu.roll(P[minus, base : base + 64, :], 63, 0)
        own(slot, 1)
        receive(slot)
        for j in range(9):
            a, c = j // 3, j % 3
            Q[9 * a + 6 + c, pl.ds(0, 8, stride=8), :] = merge(slot, 1, 0, j)
            Q[9 * a + c, pl.ds(7, 8, stride=8), :] = merge(slot, 1, 1, j)

        slot = 3 * step + 2
        for j in range(9):
            plus, minus = 3 * j + 2, 3 * j
            hi = Q[plus, 56:64, :]
            lo = Q[minus, 0:8, :]
            for x in range(8):
                if x < 7:
                    v = pltpu.roll(Q[plus, 8 * x : 8 * x + 8, :], (16 * x + 16) % LANES, 1)
                    hi = jnp.where(lane // 16 == x, v, hi)
                if x > 0:
                    v = pltpu.roll(Q[minus, 8 * x : 8 * x + 8, :], 16 * x, 1)
                    lo = jnp.where(lane // 16 == x, v, lo)
            S[slot, 0, j] = hi
            S[slot, 1, j] = lo
        send(slot)
        for j in range(9):
            plus, rest, minus = 3 * j + 2, 3 * j + 1, 3 * j
            G[0, j] = jnp.zeros((8, LANES), jnp.float32)
            G[1, j] = jnp.zeros((8, LANES), jnp.float32)
            R[rest] = Q[rest]
            v = Q[plus]
            R[plus] = jnp.where(lane64 < 16, v, pltpu.roll(v, 16, 1))
            v = Q[minus]
            R[minus] = jnp.where(lane64 >= LANES - 16, v, pltpu.roll(v, LANES - 16, 1))
        own(slot, 2)
        receive(slot)
        take_low = (lane < 16) & (tab_ref[9] != 2)
        take_high = (lane >= LANES - 16) & (tab_ref[11] != 2)
        for j in range(9):
            low = merge(slot, 2, 0, j)
            high = merge(slot, 2, 1, j)
            for x in range(8):
                at = slice(8 * x, 8 * x + 8)
                v = low if x == 0 else pltpu.roll(low, (LANES - 16 * x) % LANES, 1)
                R[3 * j + 2, at, :] = jnp.where(take_low, v, R[3 * j + 2, at, :])
                v = high if x == 7 else pltpu.roll(high, (LANES - 16 - 16 * x) % LANES, 1)
                R[3 * j, at, :] = jnp.where(take_high, v, R[3 * j, at, :])

        @pl.when(step == 0)
        def _():
            snap[...] = R[...]

        @pl.when(step == 1)
        def _():
            for i in range(27):
                snap[i] = jnp.where(lane64 % SLOTS < n_fine + n_mid, R[i], snap[i])

        return carry

    R[...] = f_ref[...]
    lax.fori_loop(0, 4, step_body, 0)
    for i in range(27):
        out_ref[i] = jnp.where(lane64 % SLOTS < n_fine, R[i], snap[i])


def to_lanes(arrays):
    k = arrays[0].shape[1]
    pad = SLOTS - sum(a.shape[0] for a in arrays)
    whole = jnp.concatenate(arrays + [jnp.ones((pad, k, 512), jnp.float32)], axis=0)
    return whole.reshape(SLOTS, k * 64, 8).transpose(1, 2, 0).reshape(k, 64, LANES)


def face_tables(tables, place):
    ids, devs = [], []
    base = 0
    for table in tables:
        count = table.shape[0]
        group = table // count
        ids.append(table - group * count + base)
        devs.append(jnp.where(table < 0, 2, group - place))
        base += count
    pad = ((0, SLOTS - base), (0, 0))
    ids = jnp.pad(jnp.concatenate(ids), pad).T
    devs = jnp.pad(jnp.concatenate(devs), pad, constant_values=2).T
    ids = jnp.clip(ids, 0, SLOTS - 1)
    ids = ids[:, None, :] + SLOTS * jnp.arange(8, dtype=jnp.int32)[None, :, None]
    devs = jnp.broadcast_to(devs[:, None, :], (6, 8, SLOTS))
    both = jnp.stack([ids, devs], axis=1).reshape(12, 1, LANES)
    return jnp.broadcast_to(both, (12, 8, LANES))


def advance_all(fields, solids, rates, tables, place):
    n = lax.axis_size("blk")
    counts = [f.shape[0] for f in fields]
    f_all = to_lanes(fields)
    keep = 1.0 - to_lanes([s[:, None, :] for s in solids])[0]
    level = [2] * counts[0] + [1] * counts[1] + [0] * (SLOTS - counts[0] - counts[1])
    rate = jnp.stack([rates[k] for k in level], axis=1)
    rate = jnp.tile(rate, (1, 8))
    vmem = pl.BlockSpec(memory_space=pltpu.VMEM)
    out = pl.pallas_call(
        functools.partial(lbm_kernel, n, counts[0], counts[1]),
        out_shape=jax.ShapeDtypeStruct((27, 64, LANES), jnp.float32),
        in_specs=[vmem] * 4,
        out_specs=vmem,
        scratch_shapes=[
            pltpu.VMEM((27, 80, LANES), jnp.float32),
            pltpu.VMEM((27, 64, LANES), jnp.float32),
            pltpu.VMEM((27, 64, LANES), jnp.float32),
            pltpu.VMEM((2, 9, 8, LANES), jnp.float32),
            pltpu.VMEM((27, 64, LANES), jnp.float32),
            pltpu.VMEM((12, 2, 9, 8, LANES), jnp.float32),
            pltpu.VMEM((12, 2, 2, 9, 8, LANES), jnp.float32),
            pltpu.SemaphoreType.DMA((12, 2)),
            pltpu.SemaphoreType.DMA((12, 2)),
        ],
        compiler_params=pltpu.CompilerParams(
            collective_id=0, has_side_effects=True, vmem_limit_bytes=32 * 1024 * 1024
        ),
    )(f_all, keep, rate, face_tables(tables, place))
    back = out.reshape(27 * 64, 8, SLOTS).transpose(2, 0, 1).reshape(SLOTS, 27, 512)
    fine, mid = counts[0], counts[0] + counts[1]
    return back[:fine], back[fine:mid], back[mid : mid + counts[2]]


def local(
    f_coarse,
    f_mid,
    f_fine,
    solid_coarse,
    solid_mid,
    solid_fine,
    rates,
    faces_coarse,
    faces_mid,
    faces_fine,
    explode_mid,
    explode_fine,
    coalesce_coarse,
    coalesce_mid,
):
    edge = C
    place = lax.axis_index("blk")
    n_coarse = f_coarse.shape[0]
    n_mid = f_mid.shape[0]
    n_fine = f_fine.shape[0]
    sent = jnp.concatenate(
        [f_coarse.reshape(1, n_coarse * 27, -1), f_mid.reshape(1, n_mid * 27, -1)], axis=1
    )
    beside_all = padded(sent, (("blk", 0),), 1)
    coarse_near = beside_all[:, : n_coarse * 27].reshape(3 * n_coarse, 27, -1)
    mid_near = beside_all[:, n_coarse * 27 :].reshape(3 * n_mid, 27, -1)
    pieces_mid = lookup(octant_table(coarse_near, edge), explode_mid, (place - 1) * n_coarse)
    pieces_fine = lookup(octant_table(mid_near, edge), explode_fine, (place - 1) * n_mid)
    mid_start = explode(f_mid, pieces_mid, explode_mid[:, 0], edge)
    fine_start = explode(f_fine, pieces_fine, explode_fine[:, 0], edge)
    solids = [solid_fine, solid_mid, solid_coarse]
    tables = [faces_fine, faces_mid, faces_coarse]
    fine_out, middle, coarse = advance_all(
        [fine_start, mid_start, f_coarse], solids, rates, tables, place
    )
    sent = jnp.concatenate(
        [
            restrict(middle, edge).reshape(1, n_mid * 27, -1),
            restrict(fine_out, edge).reshape(1, n_fine * 27, -1),
        ],
        axis=1,
    )
    near = padded(sent, (("blk", 0),), 1)
    mid_means = near[:, : n_mid * 27].reshape(3 * n_mid, 27, -1)
    fine_means = near[:, n_mid * 27 :].reshape(3 * n_fine, 27, -1)
    mid_at = jnp.clip(coalesce_coarse - (place - 1) * n_mid, 0, 3 * n_mid - 1)
    fine_at = jnp.clip(coalesce_mid - (place - 1) * n_fine, 0, 3 * n_fine - 1)
    coarse_out = assemble(coarse, mid_means[mid_at], coalesce_coarse, edge)
    mid_out = assemble(middle, fine_means[fine_at], coalesce_mid, edge)
    return (coarse_out, mid_out, fine_out)


def solution(mesh):
    placed = (
        P("blk", None, None),
        P("blk", None, None),
        P("blk", None, None),
        P("blk", None),
        P("blk", None),
        P("blk", None),
        P(),
        P("blk", None),
        P("blk", None),
        P("blk", None),
        P("blk", None),
        P("blk", None),
        P("blk", None),
        P("blk", None),
    )
    return jax.shard_map(
        local,
        mesh=mesh,
        in_specs=placed,
        out_specs=(P("blk", None, None), P("blk", None, None), P("blk", None, None)),
        check_vma=False,
    )
```

```python
import functools

import jax
import jax.numpy as jnp
from jax import lax
from jax.experimental import pallas as pl
from jax.experimental.pallas import tpu as pltpu
from jax.sharding import PartitionSpec as P

SLOTS = 16
LANES = 128
MESH = pl.DeviceIdType.MESH


def forward(f, stride):
    out = list(f)
    for i in range(27):
        if i // stride % 3 == 0:
            lo, mid, hi = f[i], f[i + stride], f[i + 2 * stride]
            both = lo + hi
            out[i] = both + mid
            out[i + stride] = hi - lo
            out[i + 2 * stride] = both
    return out


def backward(m, stride):
    out = list(m)
    for i in range(27):
        if i // stride % 3 == 0:
            m0, m1, m2 = m[i], m[i + stride], m[i + 2 * stride]
            out[i] = 0.5 * (m2 - m1)
            out[i + stride] = m0 - m2
            out[i + 2 * stride] = 0.5 * (m1 + m2)
    return out


def collide_row(f, keep, rate_ref):
    for stride in (9, 3, 1):
        f = forward(f, stride)
    rho = f[0]
    scale = keep / rho
    mu = []
    for k in (9, 3, 1):
        v = f[k] * scale
        mu.append((None, v, 1.0 / 3.0 + v * v))
    for a in range(3):
        ta = rho if a == 0 else rho * mu[0][a]
        for b in range(3):
            tb = ta if b == 0 else ta * mu[1][b]
            for c in range(3):
                t = tb if c == 0 else tb * mu[2][c]
                i = 9 * a + 3 * b + c
                f[i] = f[i] - rate_ref[i : i + 1, :] * (f[i] - t)
    for stride in (9, 3, 1):
        f = backward(f, stride)
    return f


PACKS = (0, 8, 16, 20)
OUT_PACKS = (0, 8, 16, 19)


def pick_rows(v, rows):
    return jnp.take_along_axis(v, rows, axis=0, mode="promise_in_bounds")


def pick(v, idx):
    return jnp.take_along_axis(v, idx, axis=1, mode="promise_in_bounds")


def lbm_kernel(
    n, n_fine, n_mid, f_ref, rate_ref, raw_ref, out_ref,
    P, Q, R, G, snap, S, RV, T, keep_ref, tab_ref, PK, PR, M, MR, send_sem, recv_sem,
):
    me = lax.axis_index("blk")
    right, left = lax.rem(me + 1, n), lax.rem(me + n - 1, n)
    barrier = pltpu.get_barrier_semaphore()

    @pl.when(me > 0)
    def _():
        pl.semaphore_signal(barrier, inc=1, device_id=(left,), device_id_type=MESH)

    @pl.when(me < n - 1)
    def _():
        pl.semaphore_signal(barrier, inc=1, device_id=(right,), device_id_type=MESH)

    lane = lax.broadcasted_iota(jnp.int32, (8, LANES), 1)
    lane64 = lax.broadcasted_iota(jnp.int32, (64, LANES), 1)
    row64 = lax.broadcasted_iota(jnp.int32, (64, LANES), 0) % 8

    def copies(slot, src, dst):
        out = []
        for side, target in ((0, right), (1, left)):
            out.append(
                pltpu.make_async_remote_copy(
                    src_ref=src,
                    dst_ref=dst(side),
                    send_sem=send_sem.at[slot, side],
                    recv_sem=recv_sem.at[slot, side],
                    device_id=(target,),
                    device_id_type=MESH,
                )
            )
        return out

    def faces(slot):
        return slot, S.at[slot], lambda side: RV.at[slot, side]

    def send(slot, src, dst):
        up, down = copies(slot, src, dst)

        @pl.when(me < n - 1)
        def _():
            up.start()

        @pl.when(me > 0)
        def _():
            down.start()

    def receive(slot, src, dst):
        up, down = copies(slot, src, dst)

        @pl.when(me < n - 1)
        def _():
            up.wait_send()
            down.wait_recv()

        @pl.when(me > 0)
        def _():
            down.wait_send()
            up.wait_recv()

    def own(slot, axis):
        for d in range(2):
            idx, dev = tab_ref[4 * axis + 2 * d], tab_ref[4 * axis + 2 * d + 1]
            for j in range(9):
                G[d, j] = jnp.where(dev == 0, pick(S[slot, d, j], idx), G[d, j])

    def merge(slot, axis, d, j):
        idx, dev = tab_ref[4 * axis + 2 * d], tab_ref[4 * axis + 2 * d + 1]
        g = jnp.where(dev == -1, pick(RV[slot, 0, d, j], idx), G[d, j])
        return jnp.where(dev == 1, pick(RV[slot, 1, d, j], idx), g)

    def collide_at(x):
        at = pl.ds(pl.multiple_of(8 * x, 8), 8)
        f = collide_row([R[i, at, :] for i in range(27)], keep_ref[at, :], rate_ref)
        to = pl.ds(pl.multiple_of(8 * x + 8, 8), 8)
        for i in range(27):
            P[i, to, :] = f[i]

    def step_body(step, carry):
        @pl.loop(0, 2)
        def _(k):
            collide_at(7 * k)

        slot = 3 * step
        for j in range(9):
            S[slot, 0, j] = P[18 + j, 64:72, :]
            S[slot, 1, j] = P[j, 8:16, :]

        send(*faces(slot))

        @pl.loop(1, 7)
        def _(x):
            collide_at(x)

        for j in range(9):
            G[0, j] = P[18 + j, 8:16, :]
            G[1, j] = P[j, 64:72, :]
        own(slot, 0)
        receive(*faces(slot))
        for j in range(9):
            P[18 + j, 0:8, :] = merge(slot, 0, 0, j)
            P[j, 72:80, :] = merge(slot, 0, 1, j)

        slot = 3 * step + 1
        for j in range(9):
            a, c = j // 3, j % 3
            plus, minus, base = 9 * a + 6 + c, 9 * a + c, 8 * (2 - a)
            S[slot, 0, j] = P[plus, pl.ds(base + 7, 8, stride=8), :]
            S[slot, 1, j] = P[minus, pl.ds(base, 8, stride=8), :]
        send(*faces(slot))
        for j in range(9):
            a, c = j // 3, j % 3
            plus, rest, minus, base = 9 * a + 6 + c, 9 * a + 3 + c, 9 * a + c, 8 * (2 - a)
            G[0, j] = P[plus, pl.ds(base, 8, stride=8), :]
            G[1, j] = P[minus, pl.ds(base + 7, 8, stride=8), :]
            Q[rest] = P[rest, base : base + 64, :]
            Q[plus] = pltpu.roll(P[plus, base : base + 64, :], 1, 0)
            Q[minus] = pltpu.roll(P[minus, base : base + 64, :], 63, 0)
        own(slot, 1)
        receive(*faces(slot))
        for j in range(9):
            a, c = j // 3, j % 3
            Q[9 * a + 6 + c, pl.ds(0, 8, stride=8), :] = merge(slot, 1, 0, j)
            Q[9 * a + c, pl.ds(7, 8, stride=8), :] = merge(slot, 1, 1, j)

        slot = 3 * step + 2
        for j in range(9):
            plus, minus = 3 * j + 2, 3 * j
            hi = Q[plus, 56:64, :]
            lo = Q[minus, 0:8, :]
            for x in range(8):
                if x < 7:
                    v = pltpu.roll(Q[plus, 8 * x : 8 * x + 8, :], (16 * x + 16) % LANES, 1)
                    hi = jnp.where(lane // 16 == x, v, hi)
                if x > 0:
                    v = pltpu.roll(Q[minus, 8 * x : 8 * x + 8, :], 16 * x, 1)
                    lo = jnp.where(lane // 16 == x, v, lo)
            S[slot, 0, j] = hi
            S[slot, 1, j] = lo
        send(*faces(slot))
        for j in range(9):
            plus, rest, minus = 3 * j + 2, 3 * j + 1, 3 * j
            G[0, j] = jnp.zeros((8, LANES), jnp.float32)
            G[1, j] = jnp.zeros((8, LANES), jnp.float32)
            R[rest] = Q[rest]
            v = Q[plus]
            R[plus] = jnp.where(lane64 < 16, v, pltpu.roll(v, 16, 1))
            v = Q[minus]
            R[minus] = jnp.where(lane64 >= LANES - 16, v, pltpu.roll(v, LANES - 16, 1))
        own(slot, 2)
        receive(*faces(slot))
        take_low = (lane < 16) & (tab_ref[9] != 2)
        take_high = (lane >= LANES - 16) & (tab_ref[11] != 2)
        for j in range(9):
            low = merge(slot, 2, 0, j)
            high = merge(slot, 2, 1, j)
            for x in range(8):
                at = slice(8 * x, 8 * x + 8)
                v = low if x == 0 else pltpu.roll(low, (LANES - 16 * x) % LANES, 1)
                R[3 * j + 2, at, :] = jnp.where(take_low, v, R[3 * j + 2, at, :])
                v = high if x == 7 else pltpu.roll(high, (LANES - 16 - 16 * x) % LANES, 1)
                R[3 * j, at, :] = jnp.where(take_high, v, R[3 * j, at, :])

        @pl.when(step == 0)
        def _():
            snap[...] = R[...]

        @pl.when(step == 1)
        def _():
            for i in range(27):
                snap[i] = jnp.where(lane64 % SLOTS < n_fine + n_mid, R[i], snap[i])

        return carry

    for g, start in enumerate(PACKS):
        for c in range(4):
            at = slice(LANES * c, LANES * c + LANES)
            T[g, at, :] = f_ref[SLOTS * start : SLOTS * start + LANES, at].T
    for i in range(28):
        g = min(i // 8, 3)
        p = i - PACKS[g]
        acc = None
        for z in range(8):
            v = T[g, pl.ds(z, 64, stride=8), :]
            shift = (16 * (z - p)) % LANES
            v = pltpu.roll(v, shift, 1) if shift else v
            acc = v if z == 0 else jnp.where(lane64 // 16 == z, v, acc)
        if i < 27:
            R[i] = acc
        else:
            keep_ref[...] = 1.0 - acc

    half = lane % 64
    pack = (half // 8) * 16 + 8 + half % 8

    @pl.loop(0, 27)
    def _(i):
        for xl in range(4):
            lo = pick(R[i, 8 * xl : 8 * xl + 8, :], pack)
            hi = pick(R[i, 8 * xl + 32 : 8 * xl + 40, :], pack)
            PK[i, 8 * xl : 8 * xl + 8, :] = jnp.where(lane < 64, lo, hi)

    @pl.when((me == 0) | (me == n - 1))
    def _():
        pl.semaphore_wait(barrier, 1)

    @pl.when((me > 0) & (me < n - 1))
    def _():
        pl.semaphore_wait(barrier, 2)

    parents = (12, PK, lambda side: PR.at[side])
    send(*parents)

    def code(k):
        return jnp.broadcast_to(raw_ref[k : k + 1, :], (8, LANES))

    for k in range(6):
        c = code(k)
        tab_ref[2 * k] = (c & 15) + lane - lane % SLOTS
        tab_ref[2 * k + 1] = (c >> 4) - 1
    row = lax.broadcasted_iota(jnp.int32, (8, LANES), 0)
    z_at = lane >> 4
    c, o = code(6), code(7)
    dev = (c >> 4) - 1
    idx = (o >> 2) * 64 + ((o & 1) * 4 + (z_at >> 1)) * 8 + (c & 7)
    rows = ((o >> 1) & 1) * 4 + (row >> 1)
    has = dev != 2
    rim = has & ((row == 0) | (row == 7) | (z_at == 0) | (z_at == 7))
    receive(*parents)

    @pl.loop(0, 27)
    def _(i):
        for xl in range(4):
            at = slice(8 * xl, 8 * xl + 8)
            v = pick(PK[i, at, :], idx)
            v = jnp.where(dev == -1, pick(PR[0, i, at, :], idx), v)
            v = jnp.where(dev == 1, pick(PR[1, i, at, :], idx), v)
            v = pick_rows(v, rows)
            for x in (2 * xl, 2 * xl + 1):
                to = slice(8 * x, 8 * x + 8)
                R[i, to, :] = jnp.where(has if x in (0, 7) else rim, v, R[i, to, :])

    lax.fori_loop(0, 4, step_body, 0)

    even = row % 2 == 0
    first = z_at % 2 == 0

    @pl.loop(0, 27)
    def _(i):
        Q[i] = jnp.where(lane64 % SLOTS < n_fine, R[i], snap[i])
        sums = []
        for x in range(4):
            v = Q[i, 16 * x : 16 * x + 8, :] + Q[i, 16 * x + 8 : 16 * x + 16, :]
            v = v + pltpu.roll(v, 7, 0)
            sums.append(v + pltpu.roll(v, LANES - 16, 1))
        lo = jnp.where(even, sums[0], pltpu.roll(sums[1], 1, 0))
        hi = jnp.where(even, sums[2], pltpu.roll(sums[3], 1, 0))
        M[i] = jnp.where(first, lo, pltpu.roll(hi, 16, 1)) * 0.125

    means = (13, M, lambda side: MR.at[side])
    send(*means)
    idxs, devs = [], []
    for ox in range(2):
        near = jnp.where(z_at < 4, code(8 + 4 * ox), code(9 + 4 * ox))
        far = jnp.where(z_at < 4, code(10 + 4 * ox), code(11 + 4 * ox))
        c = jnp.where(row < 4, near, far)
        idxs.append((z_at & 3) * 32 + (c & 15))
        devs.append((c >> 4) - 1)
    receive(*means)

    @pl.loop(0, 27)
    def _(i):
        spread = [
            [pick_rows(v, 2 * (row & 3) + xa) for v in (M[i], MR[0, i], MR[1, i])] for xa in range(2)
        ]
        for x in range(8):
            ox, xa, xb = x // 4, x % 2, x // 2 % 2
            at = slice(8 * x, 8 * x + 8)
            idx, dev = idxs[ox] + 16 * xb, devs[ox]
            mine, low, high = spread[xa]
            v = jnp.where(dev == 0, pick(mine, idx), Q[i, at, :])
            v = jnp.where(dev == -1, pick(low, idx), v)
            R[i, at, :] = jnp.where(dev == 1, pick(high, idx), v)

    for g, start in enumerate(OUT_PACKS):
        for z in range(8):
            acc = None
            for p in range(8):
                i = start + p
                if i < 8 * g:
                    continue
                shift = (16 * (p - z)) % LANES
                v = pltpu.roll(R[i], shift, 1) if shift else R[i]
                acc = v if acc is None else jnp.where(lane64 // 16 == p, v, acc)
            T[g, pl.ds(z, 64, stride=8), :] = acc
        skip = 8 * g - start
        for c in range(4):
            at = slice(LANES * c, LANES * c + LANES)
            out_ref[SLOTS * 8 * g : SLOTS * (start + 8), at] = T[g, at, :].T[SLOTS * skip :, :]


def codes(table, count, base, place):
    group = table // count
    return jnp.where(table < 0, 48, 16 * (group - place + 1) + table - group * count + base)


def advance_all(
    f_coarse, f_mid, f_fine, solid_coarse, solid_mid, solid_fine, rates, faces_coarse, faces_mid,
    faces_fine, explode_mid, explode_fine, coalesce_coarse, coalesce_mid,
):
    n = lax.axis_size("blk")
    place = lax.axis_index("blk")
    n2, n1, n0 = f_fine.shape[0], f_mid.shape[0], f_coarse.shape[0]
    assert n2 == 8 and n1 + n0 <= 8
    spare = SLOTS - n0 - n1 - n2

    f_all = jnp.concatenate([f_fine, f_mid, f_coarse, jnp.ones((spare, 27, 512), jnp.float32)])
    solid = jnp.concatenate([solid_fine, solid_mid, solid_coarse, jnp.zeros((spare, 512), jnp.float32)])
    f_all = jnp.concatenate([f_all, solid[:, None, :]], axis=1)
    f_all = f_all.transpose(1, 0, 2).reshape(28 * SLOTS, 512)

    faces = jnp.concatenate([
        codes(faces_fine, n2, 0, place),
        codes(faces_mid, n1, n2, place),
        codes(faces_coarse, n0, n2 + n1, place),
        jnp.full((spare, 6), 48, jnp.int32),
    ])
    parent = jnp.concatenate([
        codes(explode_fine[:, 0], n1, 0, place),
        codes(explode_mid[:, 0], n0, n1, place),
        jnp.full((n0 + spare,), 48, jnp.int32),
    ])
    octant = jnp.concatenate([explode_fine[:, 1], explode_mid[:, 1], jnp.zeros((n0 + spare,), jnp.int32)])
    child = jnp.concatenate([
        jnp.full((n2, 8), 48, jnp.int32),
        codes(coalesce_mid, n2, 0, place),
        codes(coalesce_coarse, n1, n2, place),
        jnp.full((spare, 8), 48, jnp.int32),
    ])
    raw = jnp.concatenate([faces, parent[:, None], octant[:, None], child], axis=1).T
    raw = jnp.tile(raw, (1, 8))

    slot = jnp.arange(LANES)[None, :] % SLOTS
    r0, r1, r2 = rates[0][:, None], rates[1][:, None], rates[2][:, None]
    rate = jnp.where(slot < n2, r2, jnp.where(slot < n2 + n1, r1, r0))

    vmem = pl.BlockSpec(memory_space=pltpu.VMEM)
    f32 = jnp.float32
    out = pl.pallas_call(
        functools.partial(lbm_kernel, n, n2, n1),
        out_shape=jax.ShapeDtypeStruct((27 * SLOTS, 512), f32),
        in_specs=[vmem] * 3,
        out_specs=vmem,
        scratch_shapes=[
            pltpu.VMEM((27, 80, LANES), f32),
            pltpu.VMEM((27, 64, LANES), f32),
            pltpu.VMEM((27, 64, LANES), f32),
            pltpu.VMEM((2, 9, 8, LANES), f32),
            pltpu.VMEM((27, 64, LANES), f32),
            pltpu.VMEM((12, 2, 9, 8, LANES), f32),
            pltpu.VMEM((12, 2, 2, 9, 8, LANES), f32),
            pltpu.VMEM((4, 512, LANES), f32),
            pltpu.VMEM((64, LANES), f32),
            pltpu.VMEM((12, 8, LANES), jnp.int32),
            pltpu.VMEM((27, 32, LANES), f32),
            pltpu.VMEM((2, 27, 32, LANES), f32),
            pltpu.VMEM((27, 8, LANES), f32),
            pltpu.VMEM((2, 27, 8, LANES), f32),
            pltpu.SemaphoreType.DMA((14, 2)),
            pltpu.SemaphoreType.DMA((14, 2)),
        ],
        compiler_params=pltpu.CompilerParams(
            collective_id=0, has_side_effects=True, vmem_limit_bytes=40 * 1024 * 1024
        ),
    )(f_all, rate, raw)
    out = out.reshape(27, SLOTS, 512)
    parts = [out[:, n2 + n1 : n2 + n1 + n0], out[:, n2 : n2 + n1], out[:, :n2]]
    return tuple(p.transpose(1, 0, 2) for p in parts)


def solution(mesh):
    row, table = P("blk", None, None), P("blk", None)
    return jax.shard_map(
        advance_all,
        mesh=mesh,
        in_specs=(row,) * 3 + (table,) * 3 + (P(),) + (table,) * 7,
        out_specs=(row,) * 3,
        check_vma=False,
    )
```

```python
import functools

import jax
import jax.numpy as jnp
from jax import lax
from jax.experimental import pallas as pl
from jax.experimental.pallas import tpu as pltpu
from jax.sharding import PartitionSpec as P

SLOTS = 16
LANES = 128
MESH = pl.DeviceIdType.MESH


def forward(f, stride):
    out = list(f)
    for i in range(27):
        if i // stride % 3 == 0:
            lo, mid, hi = f[i], f[i + stride], f[i + 2 * stride]
            both = lo + hi
            out[i] = both + mid
            out[i + stride] = hi - lo
            out[i + 2 * stride] = both
    return out


def backward(m, stride):
    out = list(m)
    for i in range(27):
        if i // stride % 3 == 0:
            m0, m1, m2 = m[i], m[i + stride], m[i + 2 * stride]
            out[i] = 0.5 * (m2 - m1)
            out[i + stride] = m0 - m2
            out[i + 2 * stride] = 0.5 * (m1 + m2)
    return out


def collide_row(f, keep, rate_ref):
    for stride in (9, 3, 1):
        f = forward(f, stride)
    rho = f[0]
    scale = keep / rho
    mu = []
    for k in (9, 3, 1):
        v = f[k] * scale
        mu.append((None, v, 1.0 / 3.0 + v * v))
    for a in range(3):
        ta = rho if a == 0 else rho * mu[0][a]
        for b in range(3):
            tb = ta if b == 0 else ta * mu[1][b]
            for c in range(3):
                t = tb if c == 0 else tb * mu[2][c]
                i = 9 * a + 3 * b + c
                f[i] = f[i] - rate_ref[i : i + 1, :] * (f[i] - t)
    for stride in (9, 3, 1):
        f = backward(f, stride)
    return f


PACKS = (0, 8, 16, 20)
OUT_PACKS = (0, 8, 16, 19)


def pick_rows(v, rows):
    return jnp.take_along_axis(v, rows, axis=0, mode="promise_in_bounds")


def pick(v, idx):
    return jnp.take_along_axis(v, idx, axis=1, mode="promise_in_bounds")


def lbm_kernel(
    n, n_fine, n_mid, n_coarse, f_ref, rate_ref, raw_ref, out_ref,
    P, Q, R, G, snap, S, RV, T, keep_ref, tab_ref, PK, PR, M, MR, send_sem, recv_sem,
):
    me = lax.axis_index("blk")
    right, left = lax.rem(me + 1, n), lax.rem(me + n - 1, n)
    barrier = pltpu.get_barrier_semaphore()

    @pl.when(me > 0)
    def _():
        pl.semaphore_signal(barrier, inc=1, device_id=(left,), device_id_type=MESH)

    @pl.when(me < n - 1)
    def _():
        pl.semaphore_signal(barrier, inc=1, device_id=(right,), device_id_type=MESH)

    lane = lax.broadcasted_iota(jnp.int32, (8, LANES), 1)
    lane64 = lax.broadcasted_iota(jnp.int32, (64, LANES), 1)
    row64 = lax.broadcasted_iota(jnp.int32, (64, LANES), 0) % 8

    def copies(slot, src, dst):
        out = []
        for side, target in ((0, right), (1, left)):
            out.append(
                pltpu.make_async_remote_copy(
                    src_ref=src,
                    dst_ref=dst(side),
                    send_sem=send_sem.at[slot, side],
                    recv_sem=recv_sem.at[slot, side],
                    device_id=(target,),
                    device_id_type=MESH,
                )
            )
        return out

    def faces(slot):
        return slot, S.at[slot], lambda side: RV.at[slot, side]

    def send(slot, src, dst):
        up, down = copies(slot, src, dst)

        @pl.when(me < n - 1)
        def _():
            up.start()

        @pl.when(me > 0)
        def _():
            down.start()

    def receive(slot, src, dst):
        up, down = copies(slot, src, dst)

        @pl.when(me < n - 1)
        def _():
            up.wait_send()
            down.wait_recv()

        @pl.when(me > 0)
        def _():
            down.wait_send()
            up.wait_recv()

    def own(slot, axis):
        for d in range(2):
            idx, dev = tab_ref[4 * axis + 2 * d], tab_ref[4 * axis + 2 * d + 1]
            for j in range(9):
                G[d, j] = jnp.where(dev == 0, pick(S[slot, d, j], idx), G[d, j])

    def merge(slot, axis, d, j):
        idx, dev = tab_ref[4 * axis + 2 * d], tab_ref[4 * axis + 2 * d + 1]
        g = jnp.where(dev == -1, pick(RV[slot, 0, d, j], idx), G[d, j])
        return jnp.where(dev == 1, pick(RV[slot, 1, d, j], idx), g)

    def collide_at(x):
        at = pl.ds(pl.multiple_of(8 * x, 8), 8)
        f = collide_row([R[i, at, :] for i in range(27)], keep_ref[at, :], rate_ref)
        to = pl.ds(pl.multiple_of(8 * x + 8, 8), 8)
        for i in range(27):
            P[i, to, :] = f[i]

    def step_body(step, carry):
        @pl.loop(0, 2)
        def _(k):
            collide_at(7 * k)

        slot = 3 * step
        for j in range(9):
            S[slot, 0, j] = P[18 + j, 64:72, :]
            S[slot, 1, j] = P[j, 8:16, :]

        send(*faces(slot))

        @pl.loop(1, 7)
        def _(x):
            collide_at(x)

        for j in range(9):
            G[0, j] = P[18 + j, 8:16, :]
            G[1, j] = P[j, 64:72, :]
        own(slot, 0)
        receive(*faces(slot))
        for j in range(9):
            P[18 + j, 0:8, :] = merge(slot, 0, 0, j)
            P[j, 72:80, :] = merge(slot, 0, 1, j)

        slot = 3 * step + 1
        for j in range(9):
            a, c = j // 3, j % 3
            plus, minus, base = 9 * a + 6 + c, 9 * a + c, 8 * (2 - a)
            S[slot, 0, j] = P[plus, pl.ds(base + 7, 8, stride=8), :]
            S[slot, 1, j] = P[minus, pl.ds(base, 8, stride=8), :]
        send(*faces(slot))
        for j in range(9):
            a, c = j // 3, j % 3
            plus, rest, minus, base = 9 * a + 6 + c, 9 * a + 3 + c, 9 * a + c, 8 * (2 - a)
            G[0, j] = P[plus, pl.ds(base, 8, stride=8), :]
            G[1, j] = P[minus, pl.ds(base + 7, 8, stride=8), :]
            Q[rest] = P[rest, base : base + 64, :]
            Q[plus] = pltpu.roll(P[plus, base : base + 64, :], 1, 0)
            Q[minus] = pltpu.roll(P[minus, base : base + 64, :], 63, 0)
        own(slot, 1)
        receive(*faces(slot))
        for j in range(9):
            a, c = j // 3, j % 3
            Q[9 * a + 6 + c, pl.ds(0, 8, stride=8), :] = merge(slot, 1, 0, j)
            Q[9 * a + c, pl.ds(7, 8, stride=8), :] = merge(slot, 1, 1, j)

        slot = 3 * step + 2
        for j in range(9):
            plus, minus = 3 * j + 2, 3 * j
            hi = Q[plus, 56:64, :]
            lo = Q[minus, 0:8, :]
            for x in range(8):
                if x < 7:
                    v = pltpu.roll(Q[plus, 8 * x : 8 * x + 8, :], (16 * x + 16) % LANES, 1)
                    hi = jnp.where(lane // 16 == x, v, hi)
                if x > 0:
                    v = pltpu.roll(Q[minus, 8 * x : 8 * x + 8, :], 16 * x, 1)
                    lo = jnp.where(lane // 16 == x, v, lo)
            S[slot, 0, j] = hi
            S[slot, 1, j] = lo
        send(*faces(slot))
        for j in range(9):
            plus, rest, minus = 3 * j + 2, 3 * j + 1, 3 * j
            G[0, j] = jnp.zeros((8, LANES), jnp.float32)
            G[1, j] = jnp.zeros((8, LANES), jnp.float32)
            R[rest] = Q[rest]
            v = Q[plus]
            R[plus] = jnp.where(lane64 < 16, v, pltpu.roll(v, 16, 1))
            v = Q[minus]
            R[minus] = jnp.where(lane64 >= LANES - 16, v, pltpu.roll(v, LANES - 16, 1))
        own(slot, 2)
        receive(*faces(slot))
        take_low = (lane < 16) & (tab_ref[9] != 2)
        take_high = (lane >= LANES - 16) & (tab_ref[11] != 2)
        for j in range(9):
            low = merge(slot, 2, 0, j)
            high = merge(slot, 2, 1, j)
            for x in range(8):
                at = slice(8 * x, 8 * x + 8)
                v = low if x == 0 else pltpu.roll(low, (LANES - 16 * x) % LANES, 1)
                R[3 * j + 2, at, :] = jnp.where(take_low, v, R[3 * j + 2, at, :])
                v = high if x == 7 else pltpu.roll(high, (LANES - 16 - 16 * x) % LANES, 1)
                R[3 * j, at, :] = jnp.where(take_high, v, R[3 * j, at, :])

        @pl.when(step == 0)
        def _():
            snap[...] = R[...]

        @pl.when(step == 1)
        def _():
            for i in range(27):
                snap[i] = jnp.where(lane64 % SLOTS < n_fine + n_mid, R[i], snap[i])

        return carry

    def swap(vs):
        for s in (1, 2, 4):
            low, new = (lane // 16) & s == 0, list(vs)
            for k in range(8):
                if k & s == 0:
                    a, b = vs[k], vs[k + s]
                    new[k] = jnp.where(low, a, pltpu.roll(b, 16 * s, 1))
                    new[k + s] = jnp.where(low, pltpu.roll(a, LANES - 16 * s, 1), b)
            vs = new
        return vs

    def part(slot, src, dst, g):
        at = pl.ds(8 * g, min(8, 27 - 8 * g))
        return slot + g, src.at[at], lambda side: dst.at[side, at]

    half = lane % 64
    pack = (half // 8) * 16 + 8 + half % 8
    for g, start in enumerate(PACKS):
        for c in range(4):
            at = slice(LANES * c, LANES * c + LANES)
            T[g, at, :] = f_ref[SLOTS * start : SLOTS * start + LANES, at].T
        for x in range(8):
            vs = swap([T[g, pl.ds(64 * x + z, 8, stride=8), :] for z in range(8)])
            at = slice(8 * x, 8 * x + 8)
            for p in range(8):
                if 8 * g <= start + p < 27:
                    R[start + p, at, :] = vs[p]
                elif start + p == 27:
                    keep_ref[at, :] = 1.0 - vs[p]
        for i in range(8 * g, min(8 * g + 8, 27)):
            for xl in range(4):
                lo = pick(R[i, 8 * xl : 8 * xl + 8, :], pack)
                hi = pick(R[i, 8 * xl + 32 : 8 * xl + 40, :], pack)
                PK[i, 8 * xl : 8 * xl + 8, :] = jnp.where(lane < 64, lo, hi)
        if g == 0:

            @pl.when((me == 0) | (me == n - 1))
            def _():
                pl.semaphore_wait(barrier, 1)

            @pl.when((me > 0) & (me < n - 1))
            def _():
                pl.semaphore_wait(barrier, 2)

        send(*part(12, PK, PR, g))

    slot_at = lane % SLOTS

    def raw(k):
        return jnp.broadcast_to(raw_ref[k : k + 1, :], (8, LANES))

    def by_level(values):
        return jnp.where(
            slot_at < n_fine, values[0], jnp.where(slot_at < n_fine + n_mid, values[1], values[2])
        )

    def code(v, counts, bases):
        group = by_level([v >> (k.bit_length() - 1) for k in counts])
        local = by_level([(v & (k - 1)) + b for k, b in zip(counts, bases)])
        return local, jnp.where(v < 0, 2, group - me)

    for k in range(6):
        local, dev = code(raw(k), (n_fine, n_mid, n_coarse), (0, n_fine, n_fine + n_mid))
        tab_ref[2 * k] = local + lane - slot_at
        tab_ref[2 * k + 1] = dev
    row = lax.broadcasted_iota(jnp.int32, (8, LANES), 0)
    z_at = lane >> 4
    local, dev = code(raw(6), (n_mid, n_coarse, n_coarse), (0, n_mid, 0))
    o = raw(7)
    idx = (o & 4) * 16 + ((o & 1) * 4 + (z_at >> 1)) * 8 + local
    rows = (o & 2) * 2 + (row >> 1)
    has = dev != 2
    rim = has & ((row == 0) | (row == 7) | (z_at == 0) | (z_at == 7))
    for g in range(4):
        receive(*part(12, PK, PR, g))

        @pl.loop(8 * g, min(8 * g + 8, 27))
        def _(i):
            for xl in range(4):
                at = slice(8 * xl, 8 * xl + 8)
                v = pick(PK[i, at, :], idx)
                v = jnp.where(dev == -1, pick(PR[0, i, at, :], idx), v)
                v = jnp.where(dev == 1, pick(PR[1, i, at, :], idx), v)
                v = pick_rows(v, rows)
                for x in (2 * xl, 2 * xl + 1):
                    to = slice(8 * x, 8 * x + 8)
                    R[i, to, :] = jnp.where(has if x in (0, 7) else rim, v, R[i, to, :])

    lax.fori_loop(0, 4, step_body, 0)

    even = row % 2 == 0
    first = z_at % 2 == 0

    def mean(i):
        Q[i] = jnp.where(lane64 % SLOTS < n_fine, R[i], snap[i])
        sums = []
        for x in range(4):
            v = Q[i, 16 * x : 16 * x + 8, :] + Q[i, 16 * x + 8 : 16 * x + 16, :]
            v = v + pltpu.roll(v, 7, 0)
            sums.append(v + pltpu.roll(v, LANES - 16, 1))
        lo = jnp.where(even, sums[0], pltpu.roll(sums[1], 1, 0))
        hi = jnp.where(even, sums[2], pltpu.roll(sums[3], 1, 0))
        M[i] = jnp.where(first, lo, pltpu.roll(hi, 16, 1)) * 0.125

    for g in range(4):
        pl.loop(8 * g, min(8 * g + 8, 27))(mean)
        send(*part(16, M, MR, g))

    idxs, devs = [], []
    for ox in range(2):
        near = jnp.where(z_at < 4, raw(8 + 4 * ox), raw(9 + 4 * ox))
        far = jnp.where(z_at < 4, raw(10 + 4 * ox), raw(11 + 4 * ox))
        local, dev = code(jnp.where(row < 4, near, far), (n_fine, n_fine, n_mid), (0, 0, n_fine))
        idxs.append((z_at & 3) * 32 + local)
        devs.append(dev)

    def take_means(i):
        spread = [
            [pick_rows(v, 2 * (row & 3) + xa) for v in (M[i], MR[0, i], MR[1, i])] for xa in range(2)
        ]
        for x in range(8):
            ox, xa, xb = x // 4, x % 2, x // 2 % 2
            at = slice(8 * x, 8 * x + 8)
            idx, dev = idxs[ox] + 16 * xb, devs[ox]
            mine, low, high = spread[xa]
            v = jnp.where(dev == 0, pick(mine, idx), Q[i, at, :])
            v = jnp.where(dev == -1, pick(low, idx), v)
            R[i, at, :] = jnp.where(dev == 1, pick(high, idx), v)

    for g, start in enumerate(OUT_PACKS):
        receive(*part(16, M, MR, g))
        pl.loop(8 * g, min(8 * g + 8, 27))(take_means)
        for x in range(8):
            vs = swap([R[start + p, 8 * x : 8 * x + 8, :] for p in range(8)])
            for z in range(8):
                T[g, pl.ds(64 * x + z, 8, stride=8), :] = vs[z]
        skip = 8 * g - start
        for c in range(4):
            at = slice(LANES * c, LANES * c + LANES)
            out_ref[SLOTS * 8 * g : SLOTS * (start + 8), at] = T[g, at, :].T[SLOTS * skip :, :]


def advance_all(
    f_coarse, f_mid, f_fine, solid_coarse, solid_mid, solid_fine, rates, faces_coarse, faces_mid,
    faces_fine, explode_mid, explode_fine, coalesce_coarse, coalesce_mid,
):
    n = lax.axis_size("blk")
    n2, n1, n0 = f_fine.shape[0], f_mid.shape[0], f_coarse.shape[0]
    assert n2 == 8 and n1 + n0 <= 8
    assert all(k & (k - 1) == 0 for k in (n0, n1, n2))
    spare = SLOTS - n0 - n1 - n2

    f_all = jnp.concatenate([f_fine, f_mid, f_coarse, jnp.ones((spare, 27, 512), jnp.float32)])
    solid = jnp.concatenate([solid_fine, solid_mid, solid_coarse, jnp.zeros((spare, 512), jnp.float32)])
    f_all = jnp.concatenate([f_all, solid[:, None, :]], axis=1)
    f_all = f_all.transpose(1, 0, 2).reshape(28 * SLOTS, 512)

    raw = jnp.concatenate([
        jnp.concatenate([faces_fine, explode_fine, jnp.full((n2, 8), -1, jnp.int32)], axis=1),
        jnp.concatenate([faces_mid, explode_mid, coalesce_mid], axis=1),
        jnp.concatenate([faces_coarse, jnp.full((n0, 2), -1, jnp.int32), coalesce_coarse], axis=1),
        jnp.full((spare, 16), -1, jnp.int32),
    ])
    raw = jnp.tile(raw.T, (1, 8))

    slot = jnp.arange(LANES)[None, :] % SLOTS
    r0, r1, r2 = rates[0][:, None], rates[1][:, None], rates[2][:, None]
    rate = jnp.where(slot < n2, r2, jnp.where(slot < n2 + n1, r1, r0))

    vmem = pl.BlockSpec(memory_space=pltpu.VMEM)
    f32 = jnp.float32
    out = pl.pallas_call(
        functools.partial(lbm_kernel, n, n2, n1, n0),
        out_shape=jax.ShapeDtypeStruct((27 * SLOTS, 512), f32),
        in_specs=[vmem] * 3,
        out_specs=vmem,
        scratch_shapes=[
            pltpu.VMEM((27, 80, LANES), f32),
            pltpu.VMEM((27, 64, LANES), f32),
            pltpu.VMEM((27, 64, LANES), f32),
            pltpu.VMEM((2, 9, 8, LANES), f32),
            pltpu.VMEM((27, 64, LANES), f32),
            pltpu.VMEM((12, 2, 9, 8, LANES), f32),
            pltpu.VMEM((12, 2, 2, 9, 8, LANES), f32),
            pltpu.VMEM((4, 512, LANES), f32),
            pltpu.VMEM((64, LANES), f32),
            pltpu.VMEM((12, 8, LANES), jnp.int32),
            pltpu.VMEM((27, 32, LANES), f32),
            pltpu.VMEM((2, 27, 32, LANES), f32),
            pltpu.VMEM((27, 8, LANES), f32),
            pltpu.VMEM((2, 27, 8, LANES), f32),
            pltpu.SemaphoreType.DMA((20, 2)),
            pltpu.SemaphoreType.DMA((20, 2)),
        ],
        compiler_params=pltpu.CompilerParams(
            collective_id=0, has_side_effects=True, vmem_limit_bytes=40 * 1024 * 1024
        ),
    )(f_all, rate, raw)
    out = out.reshape(27, SLOTS, 512)
    parts = [out[:, n2 + n1 : n2 + n1 + n0], out[:, n2 : n2 + n1], out[:, :n2]]
    return tuple(p.transpose(1, 0, 2) for p in parts)


def solution(mesh):
    row, table = P("blk", None, None), P("blk", None)
    return jax.shard_map(
        advance_all,
        mesh=mesh,
        in_specs=(row,) * 3 + (table,) * 3 + (P(),) + (table,) * 7,
        out_specs=(row,) * 3,
        check_vma=False,
    )
```
